32 devices in a mesh: blk: 32 (over z, y, x, core).
Axes of the slice: x: 2, y: 2, z: 4, core: 2. Of those that a mesh axis runs over, the one named last changes fastest.
Arguments:
- traces: bfloat16 [4096, 144, 128], P('blk')
- bands: int32 [64], replicated, may hold values from 0 to 7, never falling along the last dimension, each value on 1 to 16 neighbouring positions
Outputs:
- cross_spectra: bfloat16 [4096, 2, 2, 64, 128], P('blk')
The draws below stay inside these ranges and needn't reach their ends.
Inputs may be any that keep to these rules, and one draw needn't show every extreme that they name: `bands`: band numbers never fall along the bins; every band holds 1 to 16 bins and one holds exactly 16.
All inputs are finite; a program needn't handle non-finite values.
Results may differ from the reference program's by a relative error of at most 0.024.
Values may be sent and summed in bfloat16 or wider, within the bound.
No kernel may reach another device: no remote copies, remote signals or barrier semaphores. Data moves between devices by JAX's collectives and lax.ppermute only.
A program may use at most 128 MiB of HBM per device.

```python
import math
import jax
import jax.numpy as jnp
import numpy as np
from jax import lax

CH_DEV = 128
W = 144
L = 128
BINS = 64
HW = 16
RAM_HALF = 64
NBANDS = 8
BAND_MOST = 16
ROUNDS = 2
CHANNELS = 4096
N_BLK = 32


def draw_traces(key, part):
    keys = jax.random.split(jax.random.fold_in(key, 17), 4)
    top_scale = math.log(10.0)
    channel_scale = jnp.exp(jax.random.uniform(keys[0], (CHANNELS, 1, 1, 1), jnp.float32, 0.0, top_scale))
    envelope = jnp.exp(jax.random.uniform(keys[1], (CHANNELS, W, L // 16, 1), jnp.float32, math.log(0.3), math.log(3.0)))
    noise = jax.random.normal(keys[2], (CHANNELS, W, L // 16, 16), jnp.float32)
    common = 3.0 * jax.random.normal(keys[3], (1, W, L), jnp.float32)
    field = (channel_scale * envelope * noise).reshape(CHANNELS, W, L) + common
    return field.astype(jnp.bfloat16)


def profile(number_of, total, bound, slope):
    weights = [(1 << 20) // math.isqrt(grade ** slope) + 1 for grade in range(2, number_of + 1)]
    rest, counts = total - bound - (number_of - 1), [1] * (number_of - 1)
    while rest > 0:
        free = [i for i in range(number_of - 1) if counts[i] < bound]
        whole, budget = sum([weights[i] for i in free]), rest
        for i in free:
            addition = min(bound - counts[i], max(1, budget * weights[i] // whole), rest)
            counts[i] = counts[i] + addition
            rest = rest - addition
    return np.array([bound] + counts)


def ragged(key, number_of, total, limit, slope):
    if number_of == 2:
        one = jax.random.randint(key, (), max(1, total - limit), min(limit, total - 1) + 1)
        return jnp.stack([one, total - one])
    tallies = jnp.asarray(profile(number_of, total, limit, slope), jnp.int32)
    pairs = (number_of - 1) // 2
    source_of, sink = tallies[1:1 + 2 * pairs:2], tallies[2:2 + 2 * pairs:2]
    room = jnp.minimum(source_of - 1, limit - sink)
    passed = jax.random.randint(jax.random.fold_in(key, 1), (pairs,), 0, 1 << 20) % (room + 1)
    tallies = tallies.at[1:1 + 2 * pairs:2].set(source_of - passed).at[2:2 + 2 * pairs:2].set(sink + passed)
    return tallies[jax.random.permutation(jax.random.fold_in(key, 2), number_of)]


def setup_inputs(seed: int = 0) -> dict:
    arg_keys = jax.random.split(jax.random.key(seed), 3)
    traces = draw_traces(jax.random.fold_in(arg_keys[2], 71), 0)
    bands = jnp.searchsorted(jnp.cumsum(ragged(arg_keys[1], NBANDS, BINS, BAND_MOST, 0)), jnp.arange(BINS), side="right").astype(jnp.int32)
    return dict(traces=traces, bands=bands)


epsilon = 1e-05
floor_power = 0.25

def prepare(extended, first_channel, total_channels, bands, halo_width, ram_half):
    channel_count = extended.shape[0] - 2 * halo_width
    ext_rows = extended.shape[0]
    window_count = extended.shape[1]
    samples = extended.shape[2]
    bin_count = samples // 2
    inner = jnp.arange(channel_count, dtype=jnp.int32)
    outer = jnp.arange(ext_rows, dtype=jnp.int32)
    offset = outer[None, :] - inner[:, None]
    outer_position = first_channel - halo_width + outer
    inside = (outer_position >= 0) & (outer_position < total_channels)
    selector = ((offset >= 0) & (offset <= 2 * halo_width) & inside[None, :]).astype(jnp.float32)
    neighbour_count = lax.optimization_barrier(jnp.sum(selector, axis=1))
    neighbour_sum = jnp.einsum('ie,ewl->iwl', selector, extended.astype(jnp.float32))
    centred = extended[halo_width:halo_width + channel_count].astype(jnp.float32) - neighbour_sum / neighbour_count[:, None, None]
    balanced = centred.astype(jnp.bfloat16)
    magnitude = jnp.abs(balanced).astype(jnp.float32)
    sample_index = jnp.arange(samples, dtype=jnp.int32)
    ram_band = (jnp.abs(sample_index[:, None] - sample_index[None, :]) <= ram_half).astype(jnp.float32)
    ram_count = lax.optimization_barrier(jnp.sum(ram_band, axis=0))
    ram_sum = jnp.einsum('cwl,lm->cwm', magnitude, ram_band)
    envelope = ram_sum / ram_count + epsilon
    normalized = (balanced.astype(jnp.float32) / envelope).astype(jnp.bfloat16)
    frequency = jnp.arange(1, bin_count + 1, dtype=jnp.int32)
    phase_steps = frequency[:, None] * sample_index[None, :] % samples
    phase = 2.0 * math.pi / samples * phase_steps.astype(jnp.float32)
    dft_table = (jnp.concatenate([jnp.cos(phase), -jnp.sin(phase)], axis=0) / math.sqrt(samples)).astype(jnp.bfloat16)
    spectra = jnp.einsum('jl,cwl->jwc', dft_table.astype(jnp.float32), normalized.astype(jnp.float32))
    spectra = spectra.reshape(2, bin_count, window_count, channel_count)
    power_bins = spectra[0] * spectra[0] + spectra[1] * spectra[1]
    same_band = (bands[:, None] == bands[None, :]).astype(jnp.float32)
    band_matrix = same_band / lax.optimization_barrier(jnp.sum(same_band, axis=1, keepdims=True))
    band_mean = jnp.einsum('fg,gwc->fwc', band_matrix, power_bins, precision=lax.Precision.HIGHEST)
    whiten_scale = lax.rsqrt(jnp.maximum(band_mean, floor_power))
    return (spectra * whiten_scale[None]).astype(jnp.bfloat16)

def correlate(own_block, partner):
    flipped = jnp.stack([jnp.stack([partner[0], partner[1]]), jnp.stack([-partner[1], partner[0]])])
    window_count = own_block.shape[2]
    product = jnp.einsum('kfwc,okfwd->cofd', own_block.astype(jnp.float32), flipped.astype(jnp.float32))
    return (product / math.sqrt(window_count)).astype(jnp.bfloat16)

def reference(traces, bands):
    padded = jnp.pad(traces, ((HW, HW), (0, 0), (0, 0)))

    def one_block(block):
        start = (block * CH_DEV).astype(jnp.int32)
        extended = lax.dynamic_slice_in_dim(padded, start, CH_DEV + 2 * HW, 0)
        return prepare(extended, start, CHANNELS, bands, HW, RAM_HALF)
    whitened = lax.map(one_block, jnp.arange(N_BLK, dtype=jnp.int32))

    def tiles_of(block):
        own_block = whitened[block]
        results = []
        for round_index in range(ROUNDS):
            partner_index = ((block + round_index + 1) % N_BLK).astype(jnp.int32)
            results.append(correlate(own_block, whitened[partner_index]))
        return jnp.stack(results, axis=1)
    cross_tiles = lax.map(tiles_of, jnp.arange(N_BLK, dtype=jnp.int32))
    return cross_tiles.reshape(CHANNELS, ROUNDS, 2, BINS, CH_DEV)
```

```python
import functools
import math

import jax
import jax.numpy as jnp
import ml_dtypes
import numpy as np
from jax import lax
from jax.experimental import pallas as pl
from jax.experimental.pallas import tpu as pltpu
from jax.sharding import PartitionSpec as P

HW = 16
RAM_HALF = 64
ROUNDS = 2
EPSILON = 1e-05
FLOOR = 0.25

STEP = 16
BINS_STEP = 16
GROUP = 16
WINDOW_CHUNKS = (1, 2, 2, 2, 2)


def prepare_kernel(x_ref, lo_ref, hi_ref, sel_ref, inv_ref, ram_ref, raminv_ref, table_ref, band_ref, bandinv_ref,
                   out_ref, ext, wide):
    channels, step, samples = x_ref.shape
    rows = channels * step
    side = HW * step
    ext[0:side, :] = lo_ref[...].astype(jnp.float32).reshape(side, samples)
    ext[side : side + rows, :] = x_ref[...].astype(jnp.float32).reshape(rows, samples)
    ext[side + rows :, :] = hi_ref[...].astype(jnp.float32).reshape(side, samples)
    sel = sel_ref[...]
    inv = inv_ref[...]
    ram = ram_ref[...]
    raminv = raminv_ref[...]
    table = table_ref[...]
    band = band_ref[...]
    bandinv = bandinv_ref[...]
    bins = table.shape[0] // 2
    for start in range(0, step, GROUP):
        group = range(start, start + GROUP)
        around = [ext[pl.ds(w, channels + 2 * HW, stride=step), :] for w in group]
        total = jnp.dot(
            sel, jnp.concatenate([a.astype(jnp.bfloat16) for a in around], axis=1), preferred_element_type=jnp.float32
        )
        balanced = jnp.concatenate(
            [
                (a[HW : HW + channels] - total[:, n * samples : (n + 1) * samples] * inv).astype(jnp.bfloat16)
                for n, a in enumerate(around)
            ],
            axis=0,
        )
        ram_sum = jnp.dot(jnp.abs(balanced), ram, preferred_element_type=jnp.float32)
        envelope = ram_sum * raminv + EPSILON
        normalized = (balanced.astype(jnp.float32) / envelope).astype(jnp.bfloat16)
        spectra = lax.dot_general(table, normalized, (((1,), (1,)), ((), ())), preferred_element_type=jnp.float32)
        re, im = spectra[:bins], spectra[bins:]
        power = re * re + im * im
        first = power.astype(jnp.bfloat16)
        rest = power - first.astype(jnp.float32)
        second = rest.astype(jnp.bfloat16)
        third = (rest - second.astype(jnp.float32)).astype(jnp.bfloat16)
        pieces = jnp.concatenate([first, second, third], axis=0)
        band_sum = jnp.dot(band, pieces, preferred_element_type=jnp.float32)
        for n, w in enumerate(group):
            part = slice(n * channels, (n + 1) * channels)
            scale = lax.rsqrt(jnp.maximum(band_sum[:, part] * bandinv, FLOOR))
            wide[pl.ds(w, bins, stride=step), :] = re[:, part] * scale
            wide[pl.ds(bins * step + w, bins, stride=step), :] = im[:, part] * scale
    out_ref[...] = wide[...].reshape(2, bins, step, channels).astype(out_ref.dtype)


def prepare(traces, lo, hi, first, halo_first, windows, consts):
    channels, _, samples = traces.shape
    bins = samples // 2
    steps = windows // STEP
    base, side = first // STEP, (first - halo_first) // STEP
    whole = lambda a: pl.BlockSpec(a.shape, lambda i: (0,) * a.ndim)
    return pl.pallas_call(
        prepare_kernel,
        grid=(steps,),
        in_specs=[
            pl.BlockSpec((channels, STEP, samples), lambda i: (0, base + i, 0)),
            pl.BlockSpec((HW, STEP, samples), lambda i: (0, side + i, 0)),
            pl.BlockSpec((HW, STEP, samples), lambda i: (0, side + i, 0)),
        ] + [whole(a) for a in consts],
        out_specs=pl.BlockSpec((2, bins, STEP, channels), lambda i: (0, 0, i, 0)),
        out_shape=jax.ShapeDtypeStruct((2, bins, windows, channels), jnp.bfloat16),
        scratch_shapes=[
            pltpu.VMEM(((channels + 2 * HW) * STEP, samples), jnp.float32),
            pltpu.VMEM((2 * bins * STEP, channels), jnp.float32),
        ],
        compiler_params=pltpu.CompilerParams(vmem_limit_bytes=32 * 1024 * 1024),
        cost_estimate=pl.CostEstimate(
            flops=windows * 2 * channels * samples * 1600,
            bytes_accessed=windows * channels * samples * 4,
            transcendentals=0,
        ),
        name="prepare",
    )(traces, lo, hi, *consts)


def correlate_kernel(n_own, n_partner, scale, *refs):
    own = refs[:n_own]
    partner = refs[n_own : n_own + n_partner]
    out_ref, wide = refs[-2:]
    step = own[0].shape[1]
    channels = own[0].shape[3]
    for k in range(step):
        parts = []
        for group in (own, partner):
            for part in range(2):
                pieces = [ref[part, k] for ref in group]
                parts.append(pieces[0] if len(pieces) == 1 else jnp.concatenate(pieces, axis=0))
        a_re, a_im, b_re, b_im = parts
        b = jnp.concatenate([b_re, b_im], axis=1)
        dims = (((0,), (0,)), ((), ()))
        by_re = lax.dot_general(a_re, b, dims, preferred_element_type=jnp.float32)
        by_im = lax.dot_general(a_im, b, dims, preferred_element_type=jnp.float32)
        re = by_re[:, :channels] + by_im[:, channels:]
        im = by_im[:, :channels] - by_re[:, channels:]
        wide[0, pl.ds(k, channels, stride=step), :] = re * scale
        wide[1, pl.ds(k, channels, stride=step), :] = im * scale
    for part in range(2):
        out_ref[:, 0, part] = wide[part].reshape(channels, step, channels).astype(out_ref.dtype)


def correlate(own, partner, round_index, first_bin, bins, total_bins, target=None):
    channels = own[0].shape[3]
    windows = sum(a.shape[2] for a in own)
    steps = bins // BINS_STEP
    base = first_bin // BINS_STEP
    shift = base - (0 if partner[0].shape[1] == total_bins else base)
    specs = [pl.BlockSpec((2, BINS_STEP, a.shape[2], channels), lambda i: (0, base + i, 0, 0)) for a in own]
    specs += [pl.BlockSpec((2, BINS_STEP, a.shape[2], channels), lambda i: (0, shift + i, 0, 0)) for a in partner]
    operands = list(own) + list(partner)
    aliases = {}
    if target is not None:
        specs.append(pl.BlockSpec(memory_space=pl.ANY))
        aliases = {len(operands): 0}
        operands.append(target)
    return pl.pallas_call(
        functools.partial(correlate_kernel, len(own), len(partner), 1.0 / math.sqrt(windows)),
        grid=(steps,),
        in_specs=specs,
        out_specs=pl.BlockSpec((channels, 1, 2, BINS_STEP, channels), lambda i: (0, round_index, 0, base + i, 0)),
        out_shape=jax.ShapeDtypeStruct((channels, ROUNDS, 2, total_bins, channels), jnp.bfloat16),
        scratch_shapes=[pltpu.VMEM((2, channels * BINS_STEP, channels), jnp.float32)],
        input_output_aliases=aliases,
        compiler_params=pltpu.CompilerParams(vmem_limit_bytes=48 * 1024 * 1024),
        cost_estimate=pl.CostEstimate(
            flops=bins * 8 * windows * channels * channels * 4,
            bytes_accessed=bins * channels * (windows * 8 + channels * 4),
            transcendentals=0,
        ),
        name="correlate",
    )(*operands)


def constants(first_channel, total_channels, channels, samples, bands):
    bins = samples // 2
    inner, outer = np.arange(channels), np.arange(channels + 2 * HW)
    offset = outer[None, :] - inner[:, None]
    sel = ((offset >= 0) & (offset <= 2 * HW)).astype(ml_dtypes.bfloat16)
    at = first_channel + jnp.arange(channels, dtype=jnp.int32)
    count = jnp.minimum(at, HW) + jnp.minimum(total_channels - 1 - at, HW) + 1
    inv = jnp.broadcast_to((1.0 / count.astype(jnp.float32))[:, None], (channels, samples))
    sample = np.arange(samples)
    near = np.abs(sample[:, None] - sample[None, :]) <= RAM_HALF
    ram = near.astype(ml_dtypes.bfloat16)
    raminv = (1.0 / near.sum(axis=0, dtype=np.float32)).astype(np.float32)[None, :]
    phase = 2.0 * math.pi / samples * (np.arange(1, bins + 1)[:, None] * sample[None, :] % samples)
    table = (np.concatenate([np.cos(phase), -np.sin(phase)], axis=0) / math.sqrt(samples)).astype(ml_dtypes.bfloat16)
    same = bands[:, None] == bands[None, :]
    size = jnp.sum(same.astype(jnp.float32), axis=1, keepdims=True)
    band = jnp.tile(same.astype(jnp.bfloat16), (1, 3))
    bandinv = jnp.broadcast_to(1.0 / size, (bins, channels))
    return [jnp.asarray(sel), inv, jnp.asarray(ram), jnp.asarray(raminv), jnp.asarray(table), band, bandinv]


def per_device(traces, bands):
    channels, windows, samples = traces.shape
    bins = samples // 2
    count = lax.axis_size("blk")
    ends = count - 1
    up = [(i, i + 1) for i in range(ends)]
    down = [(i + 1, i) for i in range(ends)]
    first_pairs = [((i + 2) % count, i) if i % 2 == 0 else (i, i) for i in range(count)]
    second_pairs = [((i + 2) % count, i) if i % 2 == 1 else (i, i) for i in range(count)]
    swap = [(i ^ 1, i) for i in range(count)]

    starts, sizes, at = [], [], 0
    for n in WINDOW_CHUNKS:
        starts.append(at)
        sizes.append(n * STEP)
        at += n * STEP

    cuts = [(0, sizes[0]), (sizes[0], windows)]
    halos = []
    for a, b in cuts:
        lo = lax.ppermute(traces[channels - HW :, a:b], "blk", up)
        hi = lax.ppermute(traces[:HW, a:b], "blk", down)
        halos.append((lo, hi))
    consts = constants(lax.axis_index("blk") * channels, channels * count, channels, samples, bands)

    own, held, other = [], [], []
    for n, (start, size) in enumerate(zip(starts, sizes)):
        lo, hi = halos[min(n, 1)]
        if own:
            lo, hi, own[-1] = lax.optimization_barrier((lo, hi, own[-1]))
        own.append(prepare(traces, lo, hi, start, cuts[min(n, 1)][0], size, consts))
    for chunk in own:
        held.append(lax.ppermute(chunk, "blk", first_pairs))
    for chunk in held:
        other.append(lax.ppermute(chunk, "blk", swap))
    out = correlate(own, other, 0, 0, bins, bins)
    for first in range(0, bins, BINS_STEP):
        mine = jnp.concatenate([c[:, first : first + BINS_STEP] for c in held], axis=2)
        far = lax.ppermute(mine, "blk", second_pairs)
        out = correlate(own, [far], 1, first, BINS_STEP, bins, out)
    return out


def solution(mesh):
    placed = (P("blk", None, None), P())
    return jax.shard_map(
        per_device,
        mesh=mesh,
        in_specs=placed,
        out_specs=P("blk", None, None, None, None),
        check_vma=False,
    )
```

```python
import functools
import math

import jax
import jax.numpy as jnp
import ml_dtypes
import numpy as np
from jax import lax
from jax.experimental import pallas as pl
from jax.experimental.pallas import tpu as pltpu
from jax.sharding import PartitionSpec as P

HW = 16
RAM_HALF = 64
ROUNDS = 2
EPSILON = 1e-05
FLOOR = 0.25

STEP = 16
BINS_STEP = 16
GROUP = 16
VMEM = 32 * 1024 * 1024
CHUNKS = (2, 2, 2, 2, 1)
TOKEN = 1
FIRST_ROUND_AFTER = 3
AFTER = {2: 0, 3: 1}
HALO_STEPS = 4


def prepare_kernel(odd_ref, x_ref, lo_even, lo_odd, hi_even, hi_odd, sel_ref, inv_ref, ram_ref, raminv_ref,
                   table_ref, band_ref, bandinv_ref, out_ref, ext, wide):
    channels, step, samples = x_ref.shape
    rows = channels * step
    side = HW * step
    odd = odd_ref[0] != 0

    def put(at, ref):
        count = ref.shape[0] * step
        ext[at : at + count, :] = ref[...].astype(jnp.float32).reshape(count, samples)

    @pl.when(odd)
    def _():
        put(0, lo_odd)
        put(side + rows, hi_odd)

    @pl.when(jnp.logical_not(odd))
    def _():
        put(0, lo_even)
        put(side + rows, hi_even)

    put(side, x_ref)
    sel = sel_ref[...]
    inv = inv_ref[...]
    ram = ram_ref[...]
    raminv = raminv_ref[...]
    table = table_ref[...]
    band = band_ref[...]
    bandinv = bandinv_ref[...]
    bins = table.shape[0] // 2
    for start in range(0, step, GROUP):
        group = range(start, start + GROUP)
        around = [ext[pl.ds(w, channels + 2 * HW, stride=step), :] for w in group]
        total = jnp.dot(
            sel, jnp.concatenate([a.astype(jnp.bfloat16) for a in around], axis=1), preferred_element_type=jnp.float32
        )
        balanced = jnp.concatenate(
            [
                (a[HW : HW + channels] - total[:, n * samples : (n + 1) * samples] * inv).astype(jnp.bfloat16)
                for n, a in enumerate(around)
            ],
            axis=0,
        )
        ram_sum = jnp.dot(jnp.abs(balanced), ram, preferred_element_type=jnp.float32)
        envelope = ram_sum * raminv + EPSILON
        normalized = (balanced.astype(jnp.float32) / envelope).astype(jnp.bfloat16)
        spectra = lax.dot_general(table, normalized, (((1,), (1,)), ((), ())), preferred_element_type=jnp.float32)
        re, im = spectra[:bins], spectra[bins:]
        power = re * re + im * im
        first = power.astype(jnp.bfloat16)
        rest = power - first.astype(jnp.float32)
        second = rest.astype(jnp.bfloat16)
        third = (rest - second.astype(jnp.float32)).astype(jnp.bfloat16)
        pieces = jnp.concatenate([first, second, third], axis=0)
        band_sum = jnp.dot(band, pieces, preferred_element_type=jnp.float32)
        for n, w in enumerate(group):
            part = slice(n * channels, (n + 1) * channels)
            scale = lax.rsqrt(jnp.maximum(band_sum[:, part] * bandinv, FLOOR))
            wide[pl.ds(w, bins, stride=step), :] = re[:, part] * scale
            wide[pl.ds(bins * step + w, bins, stride=step), :] = im[:, part] * scale
    out_ref[...] = wide[...].reshape(2, bins, step, channels).astype(out_ref.dtype)


def borders_kernel(early, odd_ref, x_ref, first_ref, rest_ref, inner_ref, sems):
    channels, windows, _ = x_ref.shape
    late = windows - early
    top = channels - HW
    outer = odd_ref[0] * top
    inner = top - outer
    copies = [
        pltpu.make_async_copy(x_ref.at[pl.ds(outer, HW), pl.ds(0, early), :], first_ref, sems.at[0]),
        pltpu.make_async_copy(x_ref.at[pl.ds(inner, HW)], inner_ref, sems.at[1]),
        pltpu.make_async_copy(x_ref.at[pl.ds(outer, HW), pl.ds(early, late), :], rest_ref, sems.at[2]),
    ]
    for copy in copies:
        copy.start()
    for copy in copies:
        copy.wait()


def borders(traces, odd, early):
    _, windows, samples = traces.shape
    shape = lambda n: jax.ShapeDtypeStruct((HW, n, samples), traces.dtype)
    return pl.pallas_call(
        functools.partial(borders_kernel, early),
        in_specs=[pl.BlockSpec(memory_space=pltpu.SMEM), pl.BlockSpec(memory_space=pl.ANY)],
        out_specs=[pl.BlockSpec(memory_space=pltpu.VMEM)] * 3,
        out_shape=[shape(early), shape(windows - early), shape(windows)],
        scratch_shapes=[pltpu.SemaphoreType.DMA((3,))],
        cost_estimate=pl.CostEstimate(flops=1, bytes_accessed=1, transcendentals=0),
        name="borders",
    )(odd, traces)


def prepare(x, odd, halos, first, windows, consts):
    channels, _, samples = x.shape
    bins = samples // 2
    whole = lambda a: pl.BlockSpec(a.shape, lambda i: (0,) * a.ndim)
    part = lambda rows, start: pl.BlockSpec((rows, STEP, samples), lambda i: (0, start // STEP + i, 0))
    return pl.pallas_call(
        prepare_kernel,
        grid=(windows // STEP,),
        in_specs=[pl.BlockSpec(memory_space=pltpu.SMEM), part(channels, first)]
        + [part(HW, start) for _, start in halos]
        + [whole(a) for a in consts],
        out_specs=pl.BlockSpec((2, bins, STEP, channels), lambda i: (0, 0, i, 0)),
        out_shape=jax.ShapeDtypeStruct((2, bins, windows, channels), jnp.bfloat16),
        scratch_shapes=[
            pltpu.VMEM(((channels + 2 * HW) * STEP, samples), jnp.float32),
            pltpu.VMEM((2 * bins * STEP, channels), jnp.float32),
        ],
        compiler_params=pltpu.CompilerParams(vmem_limit_bytes=VMEM),
        cost_estimate=pl.CostEstimate(flops=1, bytes_accessed=1, transcendentals=0),
        name="prepare",
    )(odd, x, *[a for a, _ in halos], *consts)


def correlate_kernel(n_own, n_partner, scale, pick_ref, *refs):
    own = refs[:n_own]
    partner = refs[n_own : n_own + n_partner]
    far = refs[n_own + n_partner] if pick_ref is not None else None
    out_ref, wide = refs[-2:]
    step = own[0].shape[1]
    channels = own[0].shape[3]

    def whole(group, part, k):
        pieces = [ref[part, k] for ref in group]
        return pieces[0] if len(pieces) == 1 else jnp.concatenate(pieces, axis=0)

    def run(partner):
        for k in range(step):
            a_re, a_im = whole(own, 0, k), whole(own, 1, k)
            b = jnp.concatenate([whole(partner, 0, k), whole(partner, 1, k)], axis=1)
            dims = (((0,), (0,)), ((), ()))
            by_re = lax.dot_general(a_re, b, dims, preferred_element_type=jnp.float32)
            by_im = lax.dot_general(a_im, b, dims, preferred_element_type=jnp.float32)
            re = by_re[:, :channels] + by_im[:, channels:]
            im = by_im[:, :channels] - by_re[:, channels:]
            wide[0, pl.ds(k, channels, stride=step), :] = re * scale
            wide[1, pl.ds(k, channels, stride=step), :] = im * scale

    if far is None:
        run(partner)
    else:
        pl.when(pick_ref[0] == 0)(lambda: run(partner))
        pl.when(pick_ref[0] != 0)(lambda: run([far]))
    for part in range(2):
        out_ref[:, 0, part] = wide[part].reshape(channels, step, channels).astype(out_ref.dtype)


def correlate(own, partner, round_index, first_bin, bins, pick=None, far=None, target=None, after=None):
    _, total_bins, _, channels = own[0].shape
    windows = sum(a.shape[2] for a in own)
    steps = bins // BINS_STEP
    base = first_bin // BINS_STEP
    operands = list(own) + list(partner)
    specs = [pl.BlockSpec((2, BINS_STEP, a.shape[2], channels), lambda i: (0, base + i, 0, 0)) for a in operands]
    if far is not None:
        specs.append(pl.BlockSpec((2, BINS_STEP, windows, channels), lambda i: (0, i, 0, 0)))
        operands.append(far)
    kernel = functools.partial(correlate_kernel, len(own), len(partner), 1.0 / math.sqrt(windows))
    if pick is None:
        kernel = functools.partial(kernel, None)
    else:
        specs.insert(0, pl.BlockSpec(memory_space=pltpu.SMEM))
        operands.insert(0, pick)
    aliases = {}
    if target is not None:
        specs.append(pl.BlockSpec(memory_space=pl.ANY))
        aliases = {len(operands): 0}
        operands.append(target)
    if after is not None:
        specs.append(pl.BlockSpec(memory_space=pl.ANY))
        operands.append(after)
    return pl.pallas_call(
        kernel,
        grid=(steps,),
        in_specs=specs,
        out_specs=pl.BlockSpec((channels, 1, 2, BINS_STEP, channels), lambda i: (0, round_index, 0, base + i, 0)),
        out_shape=jax.ShapeDtypeStruct((channels, ROUNDS, 2, total_bins, channels), jnp.bfloat16),
        scratch_shapes=[pltpu.VMEM((2, channels * BINS_STEP, channels), jnp.float32)],
        input_output_aliases=aliases,
        compiler_params=pltpu.CompilerParams(vmem_limit_bytes=VMEM),
        cost_estimate=pl.CostEstimate(flops=1, bytes_accessed=1, transcendentals=0),
        name="correlate",
    )(*operands)


def edges(block, total_channels, channels, samples):
    inner, outer = np.arange(channels), np.arange(channels + 2 * HW)
    offset = outer[None, :] - inner[:, None]
    near = jnp.asarray((offset >= 0) & (offset <= 2 * HW))
    at = block * channels - HW + jnp.asarray(outer, jnp.int32)
    sel = (near & (at >= 0)[None, :] & (at < total_channels)[None, :]).astype(jnp.bfloat16)
    own = block * channels + jnp.asarray(inner, jnp.int32)
    count = jnp.minimum(own, HW) + jnp.minimum(total_channels - 1 - own, HW) + 1
    inv = jnp.broadcast_to((1.0 / count.astype(jnp.float32))[:, None], (channels, samples))
    return [sel, inv]


def tables(channels, samples, bands):
    bins = samples // 2
    sample = np.arange(samples)
    near = np.abs(sample[:, None] - sample[None, :]) <= RAM_HALF
    ram = near.astype(ml_dtypes.bfloat16)
    raminv = (1.0 / near.sum(axis=0, dtype=np.float32)).astype(np.float32)[None, :]
    phase = 2.0 * math.pi / samples * (np.arange(1, bins + 1)[:, None] * sample[None, :] % samples)
    table = (np.concatenate([np.cos(phase), -np.sin(phase)], axis=0) / math.sqrt(samples)).astype(ml_dtypes.bfloat16)
    same = bands[:, None] == bands[None, :]
    size = jnp.sum(same.astype(jnp.float32), axis=1, keepdims=True)
    band = jnp.tile(same.astype(jnp.bfloat16), (1, 3))
    bandinv = jnp.broadcast_to(1.0 / size, (bins, channels))
    return [jnp.asarray(ram), jnp.asarray(raminv), jnp.asarray(table), band, bandinv]


def per_device(traces, bands):
    channels, windows, samples = traces.shape
    bins = samples // 2
    count = lax.axis_size("blk")
    block = lax.axis_index("blk")
    pick = (block % 2).astype(jnp.int32)[None]
    swap = [(i, i ^ 1) for i in range(count)]
    cross = [(i, i + 1 if i % 2 else i - 1) for i in range(1, count - 1)]
    first_pairs = [((i + 2) % count, i) if i % 2 == 0 else (i, i) for i in range(count)]
    second_pairs = [((i + 2) % count, i) for i in range(1, count, 2)]
    early = HALO_STEPS * STEP

    outer_first, outer_rest, inner = borders(traces, pick, early)
    across_first = lax.ppermute(outer_first, "blk", cross)
    beside = lax.ppermute(inner, "blk", swap)
    across_rest = lax.ppermute(outer_rest, "blk", cross)
    consts = edges(block, channels * count, channels, samples) + tables(channels, samples, bands)

    own, held = [], []
    at = 0
    for n, size in enumerate(CHUNKS):
        if n == 1:
            across_first, across_rest, own[0] = lax.optimization_barrier((across_first, across_rest, own[0]))
        elif n > 1:
            across_rest, own[-1], held[n - 2] = lax.optimization_barrier((across_rest, own[-1], held[n - 2]))
        across, skip = (across_first, 0) if at < early else (across_rest, early)
        x, first = (traces[:, : size * STEP], 0) if n == 0 else (traces, at)
        halos = [(across, at - skip), (beside, at), (beside, at), (across, at - skip)]
        own.append(prepare(x, pick, halos, first, size * STEP, consts))
        held.append(lax.ppermute(own[-1], "blk", first_pairs))
        at += size * STEP
    token = lax.ppermute(held[TOKEN][0, 0, :STEP], "blk", swap)
    far = []
    for first in range(0, bins, BINS_STEP):
        mine = jnp.concatenate([c[:, first : first + BINS_STEP] for c in own], axis=2)
        mine, token = lax.optimization_barrier((mine, token))
        far.append(lax.ppermute(mine, "blk", second_pairs))
    other = []
    for n in range(len(held)):
        if n in AFTER:
            held[n], other[AFTER[n]] = lax.optimization_barrier((held[n], other[AFTER[n]]))
        other.append(lax.ppermute(held[n], "blk", swap))
    out = None
    for n, first in enumerate(range(0, bins, BINS_STEP)):
        if n == FIRST_ROUND_AFTER:
            out = correlate(own, other, 0, 0, bins, target=out)
        out = correlate(own, held, 1, first, BINS_STEP, pick, far[n], out, token)
    return out


def solution(mesh):
    placed = (P("blk", None, None), P())
    return jax.shard_map(
        per_device,
        mesh=mesh,
        in_specs=placed,
        out_specs=P("blk", None, None, None, None),
        check_vma=False,
    )
```

```python
import functools
import math

import jax
import jax.numpy as jnp
import ml_dtypes
import numpy as np
from jax import lax
from jax.experimental import pallas as pl
from jax.experimental.pallas import tpu as pltpu
from jax.sharding import PartitionSpec as P

HW = 16
RAM_HALF = 64
ROUNDS = 2
EPSILON = 1e-05
FLOOR = 0.25

STEP = 16
BINS_STEP = 16
PITCH = 24
GROUP = 16
VMEM = 32 * 1024 * 1024
CHUNKS = (2, 2, 2, 2, 1)
TOKEN = 1
FIRST_ROUND_AFTER = 3
AFTER = {2: 0, 3: 1}
HALO_STEPS = 4


def prepare_kernel(odd_ref, x_ref, lo_even, lo_odd, hi_even, hi_odd, sel_ref, inv_ref, ram_ref, raminv_ref,
                   table_ref, band_ref, bandinv_ref, out_ref, ext, wide):
    channels, step, samples = x_ref.shape
    odd = odd_ref[0] != 0
    ext_rows = ext.reshape(ext.shape[0] * PITCH, samples)
    wide_rows = wide.reshape(wide.shape[0] * PITCH, channels)

    def put(at, ref):
        count = ref.shape[0]
        ext[at : at + count, :step, :] = ref[...].astype(jnp.float32)

    @pl.when(odd)
    def _():
        put(0, lo_odd)
        put(HW + channels, hi_odd)

    @pl.when(jnp.logical_not(odd))
    def _():
        put(0, lo_even)
        put(HW + channels, hi_even)

    put(HW, x_ref)
    sel = sel_ref[...]
    inv = inv_ref[...]
    ram = ram_ref[...]
    raminv = raminv_ref[...]
    table = table_ref[...]
    band = band_ref[...]
    bandinv = bandinv_ref[...]
    bins = table.shape[0] // 2
    for start in range(0, step, GROUP):
        group = range(start, start + GROUP)
        around = [ext_rows[pl.ds(w, channels + 2 * HW, stride=PITCH), :] for w in group]
        total = jnp.dot(
            sel, jnp.concatenate([a.astype(jnp.bfloat16) for a in around], axis=1), preferred_element_type=jnp.float32
        )
        balanced = jnp.concatenate(
            [
                (a[HW : HW + channels] - total[:, n * samples : (n + 1) * samples] * inv).astype(jnp.bfloat16)
                for n, a in enumerate(around)
            ],
            axis=0,
        )
        ram_sum = jnp.dot(jnp.abs(balanced), ram, preferred_element_type=jnp.float32)
        envelope = ram_sum * raminv + EPSILON
        normalized = (balanced.astype(jnp.float32) / envelope).astype(jnp.bfloat16)
        spectra = lax.dot_general(table, normalized, (((1,), (1,)), ((), ())), preferred_element_type=jnp.float32)
        re, im = spectra[:bins], spectra[bins:]
        power = re * re + im * im
        first = power.astype(jnp.bfloat16)
        rest = power - first.astype(jnp.float32)
        second = rest.astype(jnp.bfloat16)
        third = (rest - second.astype(jnp.float32)).astype(jnp.bfloat16)
        pieces = jnp.concatenate([first, second, third], axis=0)
        band_sum = jnp.dot(band, pieces, preferred_element_type=jnp.float32)
        for n, w in enumerate(group):
            part = slice(n * channels, (n + 1) * channels)
            scale = lax.rsqrt(jnp.maximum(band_sum[:, part] * bandinv, FLOOR))
            wide_rows[pl.ds(w, bins, stride=PITCH), :] = re[:, part] * scale
            wide_rows[pl.ds(bins * PITCH + w, bins, stride=PITCH), :] = im[:, part] * scale
    out_ref[...] = wide[:, :step, :].reshape(2, bins, step, channels).astype(out_ref.dtype)


def borders_kernel(early, odd_ref, x_ref, first_ref, rest_ref, inner_ref, sems):
    channels, windows, _ = x_ref.shape
    late = windows - early
    top = channels - HW
    outer = odd_ref[0] * top
    inner = top - outer
    copies = [
        pltpu.make_async_copy(x_ref.at[pl.ds(outer, HW), pl.ds(0, early), :], first_ref, sems.at[0]),
        pltpu.make_async_copy(x_ref.at[pl.ds(inner, HW)], inner_ref, sems.at[1]),
        pltpu.make_async_copy(x_ref.at[pl.ds(outer, HW), pl.ds(early, late), :], rest_ref, sems.at[2]),
    ]
    for copy in copies:
        copy.start()
    for copy in copies:
        copy.wait()


def borders(traces, odd, early):
    _, windows, samples = traces.shape
    shape = lambda n: jax.ShapeDtypeStruct((HW, n, samples), traces.dtype)
    return pl.pallas_call(
        functools.partial(borders_kernel, early),
        in_specs=[pl.BlockSpec(memory_space=pltpu.SMEM), pl.BlockSpec(memory_space=pl.ANY)],
        out_specs=[pl.BlockSpec(memory_space=pltpu.VMEM)] * 3,
        out_shape=[shape(early), shape(windows - early), shape(windows)],
        scratch_shapes=[pltpu.SemaphoreType.DMA((3,))],
        cost_estimate=pl.CostEstimate(flops=1, bytes_accessed=1, transcendentals=0),
        name="borders",
    )(odd, traces)


def prepare(x, odd, halos, first, windows, consts):
    channels, _, samples = x.shape
    bins = samples // 2
    whole = lambda a: pl.BlockSpec(a.shape, lambda i: (0,) * a.ndim)
    part = lambda rows, start: pl.BlockSpec((rows, STEP, samples), lambda i: (0, start // STEP + i, 0))
    return pl.pallas_call(
        prepare_kernel,
        grid=(windows // STEP,),
        in_specs=[pl.BlockSpec(memory_space=pltpu.SMEM), part(channels, first)]
        + [part(HW, start) for _, start in halos]
        + [whole(a) for a in consts],
        out_specs=pl.BlockSpec((2, bins, STEP, channels), lambda i: (0, 0, i, 0)),
        out_shape=jax.ShapeDtypeStruct((2, bins, windows, channels), jnp.bfloat16),
        scratch_shapes=[
            pltpu.VMEM((channels + 2 * HW, PITCH, samples), jnp.float32),
            pltpu.VMEM((2 * bins, PITCH, channels), jnp.float32),
        ],
        compiler_params=pltpu.CompilerParams(vmem_limit_bytes=VMEM),
        cost_estimate=pl.CostEstimate(flops=1, bytes_accessed=1, transcendentals=0),
        name="prepare",
    )(odd, x, *[a for a, _ in halos], *consts)


def correlate_kernel(n_own, n_partner, scale, pick_ref, *refs):
    own = refs[:n_own]
    partner = refs[n_own : n_own + n_partner]
    far = refs[n_own + n_partner] if pick_ref is not None else None
    out_ref, wide = refs[-2:]
    step = own[0].shape[1]
    channels = own[0].shape[3]

    def whole(group, part, k):
        pieces = [ref[part, k] for ref in group]
        return pieces[0] if len(pieces) == 1 else jnp.concatenate(pieces, axis=0)

    def run(partner):
        for k in range(step):
            a_re, a_im = whole(own, 0, k), whole(own, 1, k)
            b = jnp.concatenate([whole(partner, 0, k), whole(partner, 1, k)], axis=1)
            dims = (((0,), (0,)), ((), ()))
            by_re = lax.dot_general(a_re, b, dims, preferred_element_type=jnp.float32)
            by_im = lax.dot_general(a_im, b, dims, preferred_element_type=jnp.float32)
            re = by_re[:, :channels] + by_im[:, channels:]
            im = by_im[:, :channels] - by_re[:, channels:]
            wide[0, pl.ds(k, channels, stride=PITCH), :] = re * scale
            wide[1, pl.ds(k, channels, stride=PITCH), :] = im * scale

    if far is None:
        run(partner)
    else:
        pl.when(pick_ref[0] == 0)(lambda: run(partner))
        pl.when(pick_ref[0] != 0)(lambda: run([far]))
    for part in range(2):
        out_ref[:, 0, part] = wide[part].reshape(channels, PITCH, channels)[:, :step].astype(out_ref.dtype)


def correlate(own, partner, round_index, first_bin, bins, pick=None, far=None, target=None, after=None):
    _, total_bins, _, channels = own[0].shape
    windows = sum(a.shape[2] for a in own)
    steps = bins // BINS_STEP
    base = first_bin // BINS_STEP
    operands = list(own) + list(partner)
    specs = [pl.BlockSpec((2, BINS_STEP, a.shape[2], channels), lambda i: (0, base + i, 0, 0)) for a in operands]
    if far is not None:
        specs.append(pl.BlockSpec((2, BINS_STEP, windows, channels), lambda i: (0, i, 0, 0)))
        operands.append(far)
    kernel = functools.partial(correlate_kernel, len(own), len(partner), 1.0 / math.sqrt(windows))
    if pick is None:
        kernel = functools.partial(kernel, None)
    else:
        specs.insert(0, pl.BlockSpec(memory_space=pltpu.SMEM))
        operands.insert(0, pick)
    aliases = {}
    if target is not None:
        specs.append(pl.BlockSpec(memory_space=pl.ANY))
        aliases = {len(operands): 0}
        operands.append(target)
    if after is not None:
        specs.append(pl.BlockSpec(memory_space=pl.ANY))
        operands.append(after)
    return pl.pallas_call(
        kernel,
        grid=(steps,),
        in_specs=specs,
        out_specs=pl.BlockSpec((channels, 1, 2, BINS_STEP, channels), lambda i: (0, round_index, 0, base + i, 0)),
        out_shape=jax.ShapeDtypeStruct((channels, ROUNDS, 2, total_bins, channels), jnp.bfloat16),
        scratch_shapes=[pltpu.VMEM((2, channels * PITCH, channels), jnp.float32)],
        input_output_aliases=aliases,
        compiler_params=pltpu.CompilerParams(vmem_limit_bytes=VMEM),
        cost_estimate=pl.CostEstimate(flops=1, bytes_accessed=1, transcendentals=0),
        name="correlate",
    )(*operands)


def correlate_chunk_kernel(n_own, n_partner, scale, first_bin, round_index, pick_ref, *refs):
    own = refs[:n_own]
    partner = refs[n_own : n_own + n_partner]
    far = refs[n_own + n_partner]
    out_ref, wide, done, sems = refs[-4:]
    _, bins, _, channels = far.shape
    pitch_rows = wide.reshape(2, channels * PITCH, channels)

    def whole(group, part, k):
        pieces = [ref[part, k] for ref in group]
        return pieces[0] if len(pieces) == 1 else jnp.concatenate(pieces, axis=0)

    def run(partner, base):
        for k in range(bins):
            a_re, a_im = whole(own, 0, first_bin + k), whole(own, 1, first_bin + k)
            b = jnp.concatenate([whole(partner, 0, base + k), whole(partner, 1, base + k)], axis=1)
            dims = (((0,), (0,)), ((), ()))
            by_re = lax.dot_general(a_re, b, dims, preferred_element_type=jnp.float32)
            by_im = lax.dot_general(a_im, b, dims, preferred_element_type=jnp.float32)
            re = by_re[:, :channels] + by_im[:, channels:]
            im = by_im[:, :channels] - by_re[:, channels:]
            pitch_rows[0, pl.ds(k, channels, stride=PITCH), :] = re * scale
            pitch_rows[1, pl.ds(k, channels, stride=PITCH), :] = im * scale

    pl.when(pick_ref[0] == 0)(lambda: run(partner, first_bin))
    pl.when(pick_ref[0] != 0)(lambda: run([far], 0))
    copies = []
    for part in range(2):
        done[part] = wide[part, :, :bins, :].astype(done.dtype)
        copies.append(
            pltpu.make_async_copy(
                done.at[part], out_ref.at[:, round_index, part, pl.ds(first_bin, bins), :], sems.at[part]
            )
        )
        copies[-1].start()
    for copy in copies:
        copy.wait()


def correlate_chunk(own, partner, round_index, first_bin, pick, far, target, after):
    _, bins, windows, channels = far.shape
    total_bins = own[0].shape[1]
    operands = [pick, *own, *partner, far]
    specs = [pl.BlockSpec(memory_space=pltpu.SMEM)]
    specs += [pl.BlockSpec(memory_space=pltpu.VMEM)] * (len(operands) - 1)
    aliases = {}
    if target is not None:
        aliases = {len(operands): 0}
        operands.append(target)
        specs.append(pl.BlockSpec(memory_space=pl.ANY))
    operands.append(after)
    specs.append(pl.BlockSpec(memory_space=pl.ANY))
    return pl.pallas_call(
        functools.partial(
            correlate_chunk_kernel, len(own), len(partner), 1.0 / math.sqrt(windows), first_bin, round_index
        ),
        in_specs=specs,
        out_specs=pl.BlockSpec(memory_space=pl.ANY),
        out_shape=jax.ShapeDtypeStruct((channels, ROUNDS, 2, total_bins, channels), jnp.bfloat16),
        scratch_shapes=[
            pltpu.VMEM((2, channels, PITCH, channels), jnp.float32),
            pltpu.VMEM((2, channels, bins, channels), jnp.bfloat16),
            pltpu.SemaphoreType.DMA((2,)),
        ],
        input_output_aliases=aliases,
        compiler_params=pltpu.CompilerParams(vmem_limit_bytes=VMEM),
        cost_estimate=pl.CostEstimate(flops=1, bytes_accessed=1, transcendentals=0),
        name="correlate_chunk",
    )(*operands)


def edges(block, total_channels, channels, samples):
    inner, outer = np.arange(channels), np.arange(channels + 2 * HW)
    offset = outer[None, :] - inner[:, None]
    near = jnp.asarray((offset >= 0) & (offset <= 2 * HW))
    at = block * channels - HW + jnp.asarray(outer, jnp.int32)
    sel = (near & (at >= 0)[None, :] & (at < total_channels)[None, :]).astype(jnp.bfloat16)
    own = block * channels + jnp.asarray(inner, jnp.int32)
    count = jnp.minimum(own, HW) + jnp.minimum(total_channels - 1 - own, HW) + 1
    inv = jnp.broadcast_to((1.0 / count.astype(jnp.float32))[:, None], (channels, samples))
    return [sel, inv]


def tables(channels, samples, bands):
    bins = samples // 2
    sample = np.arange(samples)
    near = np.abs(sample[:, None] - sample[None, :]) <= RAM_HALF
    ram = near.astype(ml_dtypes.bfloat16)
    raminv = (1.0 / near.sum(axis=0, dtype=np.float32)).astype(np.float32)[None, :]
    phase = 2.0 * math.pi / samples * (np.arange(1, bins + 1)[:, None] * sample[None, :] % samples)
    table = (np.concatenate([np.cos(phase), -np.sin(phase)], axis=0) / math.sqrt(samples)).astype(ml_dtypes.bfloat16)
    same = bands[:, None] == bands[None, :]
    size = jnp.sum(same.astype(jnp.float32), axis=1, keepdims=True)
    band = jnp.tile(same.astype(jnp.bfloat16), (1, 3))
    bandinv = jnp.broadcast_to(1.0 / size, (bins, channels))
    return [jnp.asarray(ram), jnp.asarray(raminv), jnp.asarray(table), band, bandinv]


def per_device(traces, bands):
    channels, windows, samples = traces.shape
    bins = samples // 2
    count = lax.axis_size("blk")
    block = lax.axis_index("blk")
    pick = (block % 2).astype(jnp.int32)[None]
    swap = [(i, i ^ 1) for i in range(count)]
    cross = [(i, i + 1 if i % 2 else i - 1) for i in range(1, count - 1)]
    first_pairs = [((i + 2) % count, i) if i % 2 == 0 else (i, i) for i in range(count)]
    second_pairs = [((i + 2) % count, i) for i in range(1, count, 2)]
    early = HALO_STEPS * STEP

    outer_first, outer_rest, inner = borders(traces, pick, early)
    across_first = lax.ppermute(outer_first, "blk", cross)
    beside = lax.ppermute(inner, "blk", swap)
    across_rest = lax.ppermute(outer_rest, "blk", cross)
    consts = edges(block, channels * count, channels, samples) + tables(channels, samples, bands)

    own, held = [], []
    at = 0
    for n, size in enumerate(CHUNKS):
        if n == 1:
            across_first, across_rest, own[0] = lax.optimization_barrier((across_first, across_rest, own[0]))
        elif n > 1:
            across_rest, own[-1], held[n - 2] = lax.optimization_barrier((across_rest, own[-1], held[n - 2]))
        across, skip = (across_first, 0) if at < early else (across_rest, early)
        x, first = (traces[:, : size * STEP], 0) if n == 0 else (traces, at)
        halos = [(across, at - skip), (beside, at), (beside, at), (across, at - skip)]
        own.append(prepare(x, pick, halos, first, size * STEP, consts))
        held.append(lax.ppermute(own[-1], "blk", first_pairs))
        at += size * STEP
    token = lax.ppermute(held[TOKEN][0, 0, :STEP], "blk", swap)
    far = []
    for first in range(0, bins, BINS_STEP):
        mine = jnp.concatenate([c[:, first : first + BINS_STEP] for c in own], axis=2)
        mine, token = lax.optimization_barrier((mine, token))
        far.append(lax.ppermute(mine, "blk", second_pairs))
    other = []
    for n in range(len(held)):
        if n in AFTER:
            held[n], other[AFTER[n]] = lax.optimization_barrier((held[n], other[AFTER[n]]))
        other.append(lax.ppermute(held[n], "blk", swap))
    out = None
    for n, first in enumerate(range(0, bins, BINS_STEP)):
        if n == FIRST_ROUND_AFTER:
            out = correlate(own, other, 0, 0, bins, target=out)
        out = correlate_chunk(own, held, 1, first, pick, far[n], out, token)
    return out


def solution(mesh):
    placed = (P("blk", None, None), P())
    return jax.shard_map(
        per_device,
        mesh=mesh,
        in_specs=placed,
        out_specs=P("blk", None, None, None, None),
        check_vma=False,
    )
```

```python
import functools
import math

import jax
import jax.numpy as jnp
import ml_dtypes
import numpy as np
from jax import lax
from jax.experimental import pallas as pl
from jax.experimental.pallas import tpu as pltpu
from jax.sharding import PartitionSpec as P

HW = 16
RAM_HALF = 64
ROUNDS = 2
EPSILON = 1e-05
FLOOR = 0.25

STEP = 16
BINS_STEP = 16
PITCH = 24
GROUP = 16
VMEM = 32 * 1024 * 1024
CHUNKS = (2, 2, 2, 2, 1)
TOKEN = 1
FIRST_ROUND_AFTER = 3
AFTER = {2: 0, 3: 1}
HALO_STEPS = 4


def prepare_kernel(x_ref, lo_even, lo_odd, hi_even, hi_odd, sel_ref, inv_ref, ram_ref, raminv_ref,
                   table_ref, band_ref, bandinv_ref, out_ref, ext, wide):
    channels, step, samples = x_ref.shape
    odd = lax.axis_index("blk") % 2 != 0
    ext_rows = ext.reshape(ext.shape[0] * PITCH, samples)
    wide_rows = wide.reshape(wide.shape[0] * PITCH, channels)

    def put(at, ref):
        count = ref.shape[0]
        ext[at : at + count, :step, :] = ref[...].astype(jnp.float32)

    @pl.when(odd)
    def _():
        put(0, lo_odd)
        put(HW + channels, hi_odd)

    @pl.when(jnp.logical_not(odd))
    def _():
        put(0, lo_even)
        put(HW + channels, hi_even)

    put(HW, x_ref)
    sel = sel_ref[...]
    inv = inv_ref[...]
    ram = ram_ref[...]
    raminv = raminv_ref[...]
    table = table_ref[...]
    band = band_ref[...]
    bandinv = bandinv_ref[...]
    bins = table.shape[0] // 2
    for start in range(0, step, GROUP):
        group = range(start, start + GROUP)
        around = [ext_rows[pl.ds(w, channels + 2 * HW, stride=PITCH), :] for w in group]
        total = jnp.dot(
            sel, jnp.concatenate([a.astype(jnp.bfloat16) for a in around], axis=1), preferred_element_type=jnp.float32
        )
        balanced = jnp.concatenate(
            [
                (a[HW : HW + channels] - total[:, n * samples : (n + 1) * samples] * inv).astype(jnp.bfloat16)
                for n, a in enumerate(around)
            ],
            axis=0,
        )
        ram_sum = jnp.dot(jnp.abs(balanced), ram, preferred_element_type=jnp.float32)
        envelope = ram_sum * raminv + EPSILON
        normalized = (balanced.astype(jnp.float32) / envelope).astype(jnp.bfloat16)
        spectra = lax.dot_general(table, normalized, (((1,), (1,)), ((), ())), preferred_element_type=jnp.float32)
        re, im = spectra[:bins], spectra[bins:]
        power = re * re + im * im
        first = power.astype(jnp.bfloat16)
        rest = power - first.astype(jnp.float32)
        second = rest.astype(jnp.bfloat16)
        third = (rest - second.astype(jnp.float32)).astype(jnp.bfloat16)
        pieces = jnp.concatenate([first, second, third], axis=0)
        band_sum = jnp.dot(band, pieces, preferred_element_type=jnp.float32)
        for n, w in enumerate(group):
            part = slice(n * channels, (n + 1) * channels)
            scale = lax.rsqrt(jnp.maximum(band_sum[:, part] * bandinv, FLOOR))
            wide_rows[pl.ds(w, bins, stride=PITCH), :] = re[:, part] * scale
            wide_rows[pl.ds(bins * PITCH + w, bins, stride=PITCH), :] = im[:, part] * scale
    out_ref[...] = wide[:, :step, :].reshape(2, bins, step, channels).astype(out_ref.dtype)


def borders_kernel(early, x_ref, first_ref, rest_ref, inner_ref, sems):
    channels, windows, _ = x_ref.shape
    late = windows - early
    top = channels - HW
    outer = lax.axis_index("blk") % 2 * top
    inner = top - outer
    copies = [
        pltpu.make_async_copy(x_ref.at[pl.ds(outer, HW), pl.ds(0, early), :], first_ref, sems.at[0]),
        pltpu.make_async_copy(x_ref.at[pl.ds(inner, HW)], inner_ref, sems.at[1]),
        pltpu.make_async_copy(x_ref.at[pl.ds(outer, HW), pl.ds(early, late), :], rest_ref, sems.at[2]),
    ]
    for copy in copies:
        copy.start()
    for copy in copies:
        copy.wait()


def borders(traces, early):
    _, windows, samples = traces.shape
    shape = lambda n: jax.ShapeDtypeStruct((HW, n, samples), traces.dtype)
    return pl.pallas_call(
        functools.partial(borders_kernel, early),
        in_specs=[pl.BlockSpec(memory_space=pl.ANY)],
        out_specs=[pl.BlockSpec(memory_space=pltpu.VMEM)] * 3,
        out_shape=[shape(early), shape(windows - early), shape(windows)],
        scratch_shapes=[pltpu.SemaphoreType.DMA((3,))],
        cost_estimate=pl.CostEstimate(flops=1, bytes_accessed=1, transcendentals=0),
        name="borders",
    )(traces)


def prepare(x, halos, first, windows, consts):
    channels, _, samples = x.shape
    bins = samples // 2
    whole = lambda a: pl.BlockSpec(a.shape, lambda i: (0,) * a.ndim)
    part = lambda rows, start: pl.BlockSpec((rows, STEP, samples), lambda i: (0, start // STEP + i, 0))
    return pl.pallas_call(
        prepare_kernel,
        grid=(windows // STEP,),
        in_specs=[part(channels, first)]
        + [part(HW, start) for _, start in halos]
        + [whole(a) for a in consts],
        out_specs=pl.BlockSpec((2, bins, STEP, channels), lambda i: (0, 0, i, 0)),
        out_shape=jax.ShapeDtypeStruct((2, bins, windows, channels), jnp.bfloat16),
        scratch_shapes=[
            pltpu.VMEM((channels + 2 * HW, PITCH, samples), jnp.float32),
            pltpu.VMEM((2 * bins, PITCH, channels), jnp.float32),
        ],
        compiler_params=pltpu.CompilerParams(vmem_limit_bytes=VMEM),
        cost_estimate=pl.CostEstimate(flops=1, bytes_accessed=1, transcendentals=0),
        name="prepare",
    )(x, *[a for a, _ in halos], *consts)


def correlate_kernel(n_own, scale, *refs):
    own, partner = refs[:n_own], refs[n_own : 2 * n_own]
    out_ref, wide = refs[-2:]
    step = own[0].shape[1]
    channels = own[0].shape[3]
    multiply(own, partner, 0, 0, step, scale, wide)
    for part in range(2):
        out_ref[:, 0, part] = wide[part, :, :step, :].astype(out_ref.dtype)


def multiply(own, partner, first, partner_first, bins, scale, wide):
    channels = own[0].shape[3]
    rows = wide.reshape(2, channels * PITCH, channels)
    dims = (((0,), (0,)), ((), ()))

    def whole(group, part, k):
        pieces = [ref[part, k] for ref in group]
        return pieces[0] if len(pieces) == 1 else jnp.concatenate(pieces, axis=0)

    for k in range(bins):
        a_re, a_im = whole(own, 0, first + k), whole(own, 1, first + k)
        b = jnp.concatenate([whole(partner, 0, partner_first + k), whole(partner, 1, partner_first + k)], axis=1)
        by_re = lax.dot_general(a_re, b, dims, preferred_element_type=jnp.float32)
        by_im = lax.dot_general(a_im, b, dims, preferred_element_type=jnp.float32)
        re = by_re[:, :channels] + by_im[:, channels:]
        im = by_im[:, :channels] - by_re[:, channels:]
        rows[0, pl.ds(k, channels, stride=PITCH), :] = re * scale
        rows[1, pl.ds(k, channels, stride=PITCH), :] = im * scale


def correlate(own, partner, round_index, target):
    _, total_bins, _, channels = own[0].shape
    windows = sum(a.shape[2] for a in own)
    operands = [*own, *partner, target]
    specs = [pl.BlockSpec((2, BINS_STEP, a.shape[2], channels), lambda i: (0, i, 0, 0)) for a in operands[:-1]]
    return pl.pallas_call(
        functools.partial(correlate_kernel, len(own), 1.0 / math.sqrt(windows)),
        grid=(total_bins // BINS_STEP,),
        in_specs=specs + [pl.BlockSpec(memory_space=pl.ANY)],
        out_specs=pl.BlockSpec((channels, 1, 2, BINS_STEP, channels), lambda i: (0, round_index, 0, i, 0)),
        out_shape=jax.ShapeDtypeStruct(target.shape, target.dtype),
        scratch_shapes=[pltpu.VMEM((2, channels, PITCH, channels), jnp.float32)],
        input_output_aliases={len(operands) - 1: 0},
        compiler_params=pltpu.CompilerParams(vmem_limit_bytes=VMEM),
        cost_estimate=pl.CostEstimate(flops=1, bytes_accessed=1, transcendentals=0),
        name="correlate",
    )(*operands)


def correlate_chunk_kernel(n_own, scale, first_bin, round_index, *refs):
    own, partner, far = refs[:n_own], refs[n_own : 2 * n_own], refs[2 * n_own]
    out_ref, wide, done, sems = refs[-4:]
    bins = far.shape[1]
    odd = lax.axis_index("blk") % 2 != 0
    pl.when(jnp.logical_not(odd))(lambda: multiply(own, partner, first_bin, first_bin, bins, scale, wide))
    pl.when(odd)(lambda: multiply(own, [far], first_bin, 0, bins, scale, wide))
    copies = []
    for part in range(2):
        done[part] = wide[part, :, :bins, :].astype(done.dtype)
        copies.append(
            pltpu.make_async_copy(
                done.at[part], out_ref.at[:, round_index, part, pl.ds(first_bin, bins), :], sems.at[part]
            )
        )
        copies[-1].start()
    for copy in copies:
        copy.wait()


def correlate_chunk(own, partner, round_index, first_bin, far, target, after):
    _, bins, windows, channels = far.shape
    total_bins = own[0].shape[1]
    operands = [*own, *partner, far]
    specs = [pl.BlockSpec(memory_space=pltpu.VMEM)] * len(operands)
    aliases = {}
    if target is not None:
        aliases = {len(operands): 0}
        operands.append(target)
        specs.append(pl.BlockSpec(memory_space=pl.ANY))
    operands.append(after)
    specs.append(pl.BlockSpec(memory_space=pl.ANY))
    return pl.pallas_call(
        functools.partial(
            correlate_chunk_kernel, len(own), 1.0 / math.sqrt(windows), first_bin, round_index
        ),
        in_specs=specs,
        out_specs=pl.BlockSpec(memory_space=pl.ANY),
        out_shape=jax.ShapeDtypeStruct((channels, ROUNDS, 2, total_bins, channels), jnp.bfloat16),
        scratch_shapes=[
            pltpu.VMEM((2, channels, PITCH, channels), jnp.float32),
            pltpu.VMEM((2, channels, bins, channels), jnp.bfloat16),
            pltpu.SemaphoreType.DMA((2,)),
        ],
        input_output_aliases=aliases,
        compiler_params=pltpu.CompilerParams(vmem_limit_bytes=VMEM),
        cost_estimate=pl.CostEstimate(flops=1, bytes_accessed=1, transcendentals=0),
        name="correlate_chunk",
    )(*operands)


def edges(block, total_channels, channels, samples):
    inner, outer = np.arange(channels), np.arange(channels + 2 * HW)
    offset = outer[None, :] - inner[:, None]
    near = jnp.asarray((offset >= 0) & (offset <= 2 * HW))
    at = block * channels - HW + jnp.asarray(outer, jnp.int32)
    sel = (near & (at >= 0)[None, :] & (at < total_channels)[None, :]).astype(jnp.bfloat16)
    own = block * channels + jnp.asarray(inner, jnp.int32)
    count = jnp.minimum(own, HW) + jnp.minimum(total_channels - 1 - own, HW) + 1
    inv = jnp.broadcast_to((1.0 / count.astype(jnp.float32))[:, None], (channels, samples))
    return [sel, inv]


def tables(channels, samples, bands):
    bins = samples // 2
    sample = np.arange(samples)
    near = np.abs(sample[:, None] - sample[None, :]) <= RAM_HALF
    ram = near.astype(ml_dtypes.bfloat16)
    raminv = (1.0 / near.sum(axis=0, dtype=np.float32)).astype(np.float32)[None, :]
    phase = 2.0 * math.pi / samples * (np.arange(1, bins + 1)[:, None] * sample[None, :] % samples)
    table = (np.concatenate([np.cos(phase), -np.sin(phase)], axis=0) / math.sqrt(samples)).astype(ml_dtypes.bfloat16)
    same = bands[:, None] == bands[None, :]
    size = jnp.sum(same.astype(jnp.float32), axis=1, keepdims=True)
    band = jnp.tile(same.astype(jnp.bfloat16), (1, 3))
    bandinv = jnp.broadcast_to(1.0 / size, (bins, channels))
    return [jnp.asarray(ram), jnp.asarray(raminv), jnp.asarray(table), band, bandinv]


def per_device(traces, bands):
    channels, windows, samples = traces.shape
    bins = samples // 2
    count = lax.axis_size("blk")
    block = lax.axis_index("blk")
    swap = [(i, i ^ 1) for i in range(count)]
    cross = [(i, i + 1 if i % 2 else i - 1) for i in range(1, count - 1)]
    first_pairs = [((i + 2) % count, i) if i % 2 == 0 else (i, i) for i in range(count)]
    second_pairs = [((i + 2) % count, i) for i in range(1, count, 2)]
    early = HALO_STEPS * STEP

    outer_first, outer_rest, inner = borders(traces, early)
    above_first = lax.ppermute(outer_first, "blk", [(i + 1, i) for i in range(1, count - 1, 2)])
    below_first = lax.ppermute(outer_first, "blk", [(i, i + 1) for i in range(1, count - 1, 2)])
    beside = lax.ppermute(inner, "blk", swap)
    across_rest = lax.ppermute(outer_rest, "blk", cross)
    consts = edges(block, channels * count, channels, samples) + tables(channels, samples, bands)

    own, held = [], []
    at = 0
    for n, size in enumerate(CHUNKS):
        if n == 1:
            below_first, across_rest, own[0] = lax.optimization_barrier((below_first, across_rest, own[0]))
        elif n > 1:
            across_rest, own[-1], held[n - 2] = lax.optimization_barrier((across_rest, own[-1], held[n - 2]))
        if at < early:
            halos = [(below_first, at), (beside, at), (beside, at), (above_first, at)]
        else:
            halos = [(across_rest, at - early), (beside, at), (beside, at), (across_rest, at - early)]
        x, first = (traces[:, : size * STEP], 0) if n == 0 else (traces, at)
        own.append(prepare(x, halos, first, size * STEP, consts))
        held.append(lax.ppermute(own[-1], "blk", first_pairs))
        at += size * STEP
    token = lax.ppermute(held[TOKEN][0, 0, :STEP], "blk", swap)
    far = []
    for first in range(0, bins, BINS_STEP):
        mine = jnp.concatenate([c[:, first : first + BINS_STEP] for c in own], axis=2)
        mine, token = lax.optimization_barrier((mine, token))
        far.append(lax.ppermute(mine, "blk", second_pairs))
    other = []
    for n in range(len(held)):
        if n in AFTER:
            held[n], other[AFTER[n]] = lax.optimization_barrier((held[n], other[AFTER[n]]))
        other.append(lax.ppermute(held[n], "blk", swap))
    out = None
    for n, first in enumerate(range(0, bins, BINS_STEP)):
        if n == FIRST_ROUND_AFTER:
            out = correlate(own, other, 0, out)
        out = correlate_chunk(own, held, 1, first, far[n], out, token)
    return out


def solution(mesh):
    placed = (P("blk", None, None), P())
    return jax.shard_map(
        per_device,
        mesh=mesh,
        in_specs=placed,
        out_specs=P("blk", None, None, None, None),
        check_vma=False,
    )
```

```python
import functools
import math

import jax
import jax.numpy as jnp
import ml_dtypes
import numpy as np
from jax import lax
from jax.experimental import pallas as pl
from jax.experimental.pallas import tpu as pltpu
from jax.sharding import PartitionSpec as P

HW = 16
RAM_HALF = 64
ROUNDS = 2
EPSILON = 1e-05
FLOOR = 0.25

STEP = 16
BINS_STEP = 16
PITCH = 24
GROUP = 16
VMEM = 32 * 1024 * 1024
CHUNKS = (2, 2, 2, 2, 1)
TOKEN = 0
FIRST_ROUND_AFTER = 3
AFTER = {2: 0, 3: 1}
HALO_STEPS = 4


def prepare_kernel(begin, offsets, x_ref, lo_even, lo_odd, hi_even, hi_odd, sel_ref, inv_ref, ram_ref, raminv_ref,
                   table_ref, band_ref, bandinv_ref, out_ref, ext, wide):
    channels, _, samples = x_ref.shape
    windows = out_ref.shape[2]
    step = STEP
    odd = lax.axis_index("blk") % 2 != 0
    ext_rows = ext.reshape(ext.shape[0] * PITCH, samples)
    wide_rows = wide.reshape(wide.shape[0] * PITCH, channels)

    def put(at, ref, window):
        count = ref.shape[0]
        ext[at : at + count, :step, :] = ref[:, window : window + step, :].astype(jnp.float32)

    sel = sel_ref[...]
    inv = inv_ref[...]
    ram = ram_ref[...]
    raminv = raminv_ref[...]
    table = table_ref[...]
    band = band_ref[...]
    bandinv = bandinv_ref[...]
    bins = table.shape[0] // 2
    for done in range(0, windows, step):

        @pl.when(odd)
        def _():
            put(0, lo_odd, offsets[1] + done)
            put(HW + channels, hi_odd, offsets[3] + done)

        @pl.when(jnp.logical_not(odd))
        def _():
            put(0, lo_even, offsets[0] + done)
            put(HW + channels, hi_even, offsets[2] + done)

        put(HW, x_ref, begin + done)
        for start in range(0, step, GROUP):
            group = range(start, start + GROUP)
            around = [ext_rows[pl.ds(w, channels + 2 * HW, stride=PITCH), :] for w in group]
            total = jnp.dot(
                sel, jnp.concatenate([a.astype(jnp.bfloat16) for a in around], axis=1), preferred_element_type=jnp.float32
            )
            balanced = jnp.concatenate(
                [
                    (a[HW : HW + channels] - total[:, n * samples : (n + 1) * samples] * inv).astype(jnp.bfloat16)
                    for n, a in enumerate(around)
                ],
                axis=0,
            )
            ram_sum = jnp.dot(jnp.abs(balanced), ram, preferred_element_type=jnp.float32)
            envelope = ram_sum * raminv + EPSILON
            normalized = (balanced.astype(jnp.float32) / envelope).astype(jnp.bfloat16)
            spectra = lax.dot_general(table, normalized, (((1,), (1,)), ((), ())), preferred_element_type=jnp.float32)
            re, im = spectra[:bins], spectra[bins:]
            power = re * re + im * im
            first = power.astype(jnp.bfloat16)
            rest = power - first.astype(jnp.float32)
            second = rest.astype(jnp.bfloat16)
            third = (rest - second.astype(jnp.float32)).astype(jnp.bfloat16)
            pieces = jnp.concatenate([first, second, third], axis=0)
            band_sum = jnp.dot(band, pieces, preferred_element_type=jnp.float32)
            for n, w in enumerate(group):
                part = slice(n * channels, (n + 1) * channels)
                scale = lax.rsqrt(jnp.maximum(band_sum[:, part] * bandinv, FLOOR))
                wide_rows[pl.ds(w, bins, stride=PITCH), :] = re[:, part] * scale
                wide_rows[pl.ds(bins * PITCH + w, bins, stride=PITCH), :] = im[:, part] * scale
        out_ref[:, :, done : done + step, :] = wide[:, :step, :].reshape(2, bins, step, channels).astype(out_ref.dtype)


def borders_kernel(early, x_ref, first_ref, rest_ref, inner_ref, sems):
    channels, windows, _ = x_ref.shape
    late = windows - early
    top = channels - HW
    outer = lax.axis_index("blk") % 2 * top
    inner = top - outer
    copies = [
        pltpu.make_async_copy(x_ref.at[pl.ds(outer, HW), pl.ds(0, early), :], first_ref, sems.at[0]),
        pltpu.make_async_copy(x_ref.at[pl.ds(inner, HW)], inner_ref, sems.at[1]),
        pltpu.make_async_copy(x_ref.at[pl.ds(outer, HW), pl.ds(early, late), :], rest_ref, sems.at[2]),
    ]
    for copy in copies:
        copy.start()
    for copy in copies:
        copy.wait()


def borders(traces, early):
    _, windows, samples = traces.shape
    shape = lambda n: jax.ShapeDtypeStruct((HW, n, samples), traces.dtype)
    return pl.pallas_call(
        functools.partial(borders_kernel, early),
        in_specs=[pl.BlockSpec(memory_space=pl.ANY)],
        out_specs=[pl.BlockSpec(memory_space=pltpu.VMEM)] * 3,
        out_shape=[shape(early), shape(windows - early), shape(windows)],
        scratch_shapes=[pltpu.SemaphoreType.DMA((3,))],
        cost_estimate=pl.CostEstimate(flops=1, bytes_accessed=1, transcendentals=0),
        name="borders",
    )(traces)


def prepare(x, halos, first, windows, consts):
    channels, _, samples = x.shape
    bins = samples // 2
    operands = [x, *[a for a, _ in halos], *consts]
    inside = pl.BlockSpec(memory_space=pltpu.VMEM)
    return pl.pallas_call(
        functools.partial(prepare_kernel, first, [start for _, start in halos]),
        in_specs=[inside] * len(operands),
        out_specs=inside,
        out_shape=jax.ShapeDtypeStruct((2, bins, windows, channels), jnp.bfloat16),
        scratch_shapes=[
            pltpu.VMEM((channels + 2 * HW, PITCH, samples), jnp.float32),
            pltpu.VMEM((2 * bins, PITCH, channels), jnp.float32),
        ],
        compiler_params=pltpu.CompilerParams(vmem_limit_bytes=VMEM),
        cost_estimate=pl.CostEstimate(flops=1, bytes_accessed=1, transcendentals=0),
        name="prepare",
    )(*operands)


def correlate_kernel(n_own, scale, *refs):
    own, partner = refs[:n_own], refs[n_own : 2 * n_own]
    out_ref, wide = refs[-2:]
    step = own[0].shape[1]
    channels = own[0].shape[3]
    multiply(own, partner, 0, 0, step, scale, wide)
    for part in range(2):
        out_ref[:, 0, part] = wide[part, :, :step, :].astype(out_ref.dtype)


def multiply(own, partner, first, partner_first, bins, scale, wide):
    channels = own[0].shape[3]
    rows = wide.reshape(2, channels * PITCH, channels)
    dims = (((0,), (0,)), ((), ()))

    def whole(group, part, k):
        pieces = [ref[part, k] for ref in group]
        return pieces[0] if len(pieces) == 1 else jnp.concatenate(pieces, axis=0)

    for k in range(bins):
        a_re, a_im = whole(own, 0, first + k), whole(own, 1, first + k)
        b = jnp.concatenate([whole(partner, 0, partner_first + k), whole(partner, 1, partner_first + k)], axis=1)
        by_re = lax.dot_general(a_re, b, dims, preferred_element_type=jnp.float32)
        by_im = lax.dot_general(a_im, b, dims, preferred_element_type=jnp.float32)
        re = by_re[:, :channels] + by_im[:, channels:]
        im = by_im[:, :channels] - by_re[:, channels:]
        rows[0, pl.ds(k, channels, stride=PITCH), :] = re * scale
        rows[1, pl.ds(k, channels, stride=PITCH), :] = im * scale


def correlate(own, partner, round_index, target):
    _, total_bins, _, channels = own[0].shape
    windows = sum(a.shape[2] for a in own)
    operands = [*own, *partner, target]
    specs = [pl.BlockSpec((2, BINS_STEP, a.shape[2], channels), lambda i: (0, i, 0, 0)) for a in operands[:-1]]
    return pl.pallas_call(
        functools.partial(correlate_kernel, len(own), 1.0 / math.sqrt(windows)),
        grid=(total_bins // BINS_STEP,),
        in_specs=specs + [pl.BlockSpec(memory_space=pl.ANY)],
        out_specs=pl.BlockSpec((channels, 1, 2, BINS_STEP, channels), lambda i: (0, round_index, 0, i, 0)),
        out_shape=jax.ShapeDtypeStruct(target.shape, target.dtype),
        scratch_shapes=[pltpu.VMEM((2, channels, PITCH, channels), jnp.float32)],
        input_output_aliases={len(operands) - 1: 0},
        compiler_params=pltpu.CompilerParams(vmem_limit_bytes=VMEM),
        cost_estimate=pl.CostEstimate(flops=1, bytes_accessed=1, transcendentals=0),
        name="correlate",
    )(*operands)


def correlate_chunk_kernel(n_own, scale, first_bin, round_index, *refs):
    own, partner, far = refs[:n_own], refs[n_own : 2 * n_own], refs[2 * n_own]
    out_ref, wide, done, sems = refs[-4:]
    bins = far.shape[1]
    odd = lax.axis_index("blk") % 2 != 0
    pl.when(jnp.logical_not(odd))(lambda: multiply(own, partner, first_bin, first_bin, bins, scale, wide))
    pl.when(odd)(lambda: multiply(own, [far], first_bin, 0, bins, scale, wide))
    copies = []
    for part in range(2):
        done[part] = wide[part, :, :bins, :].astype(done.dtype)
        copies.append(
            pltpu.make_async_copy(
                done.at[part], out_ref.at[:, round_index, part, pl.ds(first_bin, bins), :], sems.at[part]
            )
        )
        copies[-1].start()
    for copy in copies:
        copy.wait()


def correlate_chunk(own, partner, round_index, first_bin, far, target, after):
    _, bins, windows, channels = far.shape
    total_bins = own[0].shape[1]
    operands = [*own, *partner, far]
    specs = [pl.BlockSpec(memory_space=pltpu.VMEM)] * len(operands)
    aliases = {}
    if target is not None:
        aliases = {len(operands): 0}
        operands.append(target)
        specs.append(pl.BlockSpec(memory_space=pl.ANY))
    operands.append(after)
    specs.append(pl.BlockSpec(memory_space=pl.ANY))
    return pl.pallas_call(
        functools.partial(
            correlate_chunk_kernel, len(own), 1.0 / math.sqrt(windows), first_bin, round_index
        ),
        in_specs=specs,
        out_specs=pl.BlockSpec(memory_space=pl.ANY),
        out_shape=jax.ShapeDtypeStruct((channels, ROUNDS, 2, total_bins, channels), jnp.bfloat16),
        scratch_shapes=[
            pltpu.VMEM((2, channels, PITCH, channels), jnp.float32),
            pltpu.VMEM((2, channels, bins, channels), jnp.bfloat16),
            pltpu.SemaphoreType.DMA((2,)),
        ],
        input_output_aliases=aliases,
        compiler_params=pltpu.CompilerParams(vmem_limit_bytes=VMEM),
        cost_estimate=pl.CostEstimate(flops=1, bytes_accessed=1, transcendentals=0),
        name="correlate_chunk",
    )(*operands)


def edges(block, total_channels, channels, samples):
    inner, outer = np.arange(channels), np.arange(channels + 2 * HW)
    offset = outer[None, :] - inner[:, None]
    near = jnp.asarray((offset >= 0) & (offset <= 2 * HW))
    at = block * channels - HW + jnp.asarray(outer, jnp.int32)
    sel = (near & (at >= 0)[None, :] & (at < total_channels)[None, :]).astype(jnp.bfloat16)
    own = block * channels + jnp.asarray(inner, jnp.int32)
    count = jnp.minimum(own, HW) + jnp.minimum(total_channels - 1 - own, HW) + 1
    inv = jnp.broadcast_to((1.0 / count.astype(jnp.float32))[:, None], (channels, samples))
    return [sel, inv]


def tables(channels, samples, bands):
    bins = samples // 2
    sample = np.arange(samples)
    near = np.abs(sample[:, None] - sample[None, :]) <= RAM_HALF
    ram = near.astype(ml_dtypes.bfloat16)
    raminv = (1.0 / near.sum(axis=0, dtype=np.float32)).astype(np.float32)[None, :]
    phase = 2.0 * math.pi / samples * (np.arange(1, bins + 1)[:, None] * sample[None, :] % samples)
    table = (np.concatenate([np.cos(phase), -np.sin(phase)], axis=0) / math.sqrt(samples)).astype(ml_dtypes.bfloat16)
    same = bands[:, None] == bands[None, :]
    size = jnp.sum(same.astype(jnp.float32), axis=1, keepdims=True)
    band = jnp.tile(same.astype(jnp.bfloat16), (1, 3))
    bandinv = jnp.broadcast_to(1.0 / size, (bins, channels))
    return [jnp.asarray(ram), jnp.asarray(raminv), jnp.asarray(table), band, bandinv]


def per_device(traces, bands):
    channels, windows, samples = traces.shape
    bins = samples // 2
    count = lax.axis_size("blk")
    block = lax.axis_index("blk")
    swap = [(i, i ^ 1) for i in range(count)]
    cross = [(i, i + 1 if i % 2 else i - 1) for i in range(1, count - 1)]
    first_pairs = [((i + 2) % count, i) if i % 2 == 0 else (i, i) for i in range(count)]
    second_pairs = [((i + 2) % count, i) for i in range(1, count, 2)]
    early = HALO_STEPS * STEP

    outer_first, outer_rest, inner = borders(traces, early)
    above_first = lax.ppermute(outer_first, "blk", [(i + 1, i) for i in range(1, count - 1, 2)])
    below_first = lax.ppermute(outer_first, "blk", [(i, i + 1) for i in range(1, count - 1, 2)])
    beside = lax.ppermute(inner, "blk", swap)
    across_rest = lax.ppermute(outer_rest, "blk", cross)
    consts = edges(block, channels * count, channels, samples) + tables(channels, samples, bands)

    own, held = [], []
    at = 0
    for n, size in enumerate(CHUNKS):
        if n == 1:
            below_first, across_rest, own[0] = lax.optimization_barrier((below_first, across_rest, own[0]))
        elif n > 1:
            across_rest, own[-1], held[n - 2] = lax.optimization_barrier((across_rest, own[-1], held[n - 2]))
        if at < early:
            halos = [(below_first, at), (beside, at), (beside, at), (above_first, at)]
        else:
            halos = [(across_rest, at - early), (beside, at), (beside, at), (across_rest, at - early)]
        x, first = (traces[:, : size * STEP], 0) if n == 0 else (traces, at)
        own.append(prepare(x, halos, first, size * STEP, consts))
        held.append(lax.ppermute(own[-1], "blk", first_pairs))
        at += size * STEP
    token = lax.ppermute(held[TOKEN][0, 0, :STEP], "blk", swap)
    far = []
    for first in range(0, bins, BINS_STEP):
        mine = jnp.concatenate([c[:, first : first + BINS_STEP] for c in own], axis=2)
        mine, token = lax.optimization_barrier((mine, token))
        far.append(lax.ppermute(mine, "blk", second_pairs))
    other = []
    for n in range(len(held)):
        if n in AFTER:
            held[n], other[AFTER[n]] = lax.optimization_barrier((held[n], other[AFTER[n]]))
        other.append(lax.ppermute(held[n], "blk", swap))
    out = None
    for n, first in enumerate(range(0, bins, BINS_STEP)):
        if n == FIRST_ROUND_AFTER:
            out = correlate(own, other, 0, out)
        out = correlate_chunk(own, held, 1, first, far[n], out, token)
    return out


def solution(mesh):
    placed = (P("blk", None, None), P())
    return jax.shard_map(
        per_device,
        mesh=mesh,
        in_specs=placed,
        out_specs=P("blk", None, None, None, None),
        check_vma=False,
    )
```

```python
import functools
import math

import jax
import jax.numpy as jnp
import ml_dtypes
import numpy as np
from jax import lax
from jax.experimental import pallas as pl
from jax.experimental.pallas import tpu as pltpu
from jax.sharding import PartitionSpec as P

HW = 16
RAM_HALF = 64
ROUNDS = 2
EPSILON = 1e-05
FLOOR = 0.25

STEP = 16
BINS_STEP = 16
PITCH = 24
GROUP = 16
VMEM = 32 * 1024 * 1024
CHUNKS = (2, 2, 2, 2, 1)
TOKEN = 0
FIRST_ROUND_AFTER = 3
AFTER = {2: 0, 3: 1}
HALO_STEPS = 4


def prepare_kernel(begin, offsets, x_ref, lo_even, lo_odd, hi_even, hi_odd, sel_ref, inv_ref, ram_ref, raminv_ref,
                   table_ref, band_ref, bandinv_ref, out_ref, ext, wide):
    channels, _, samples = x_ref.shape
    windows = out_ref.shape[2]
    step = STEP
    odd = lax.axis_index("blk") % 2 != 0
    ext_rows = ext.reshape(ext.shape[0] * PITCH, samples)
    wide_rows = wide.reshape(wide.shape[0] * PITCH, channels)

    def put(at, ref, window):
        count = ref.shape[0]
        ext[at : at + count, :step, :] = ref[:, window : window + step, :].astype(jnp.float32)

    sel = sel_ref[...]
    inv = inv_ref[...]
    ram = ram_ref[...]
    raminv = raminv_ref[...]
    table = table_ref[...]
    band = band_ref[...]
    bandinv = bandinv_ref[...]
    bins = table.shape[0] // 2
    for done in range(0, windows, step):

        @pl.when(odd)
        def _():
            put(0, lo_odd, offsets[1] + done)
            put(HW + channels, hi_odd, offsets[3] + done)

        @pl.when(jnp.logical_not(odd))
        def _():
            put(0, lo_even, offsets[0] + done)
            put(HW + channels, hi_even, offsets[2] + done)

        put(HW, x_ref, begin + done)
        for start in range(0, step, GROUP):
            group = range(start, start + GROUP)
            around = [ext_rows[pl.ds(w, channels + 2 * HW, stride=PITCH), :] for w in group]
            total = jnp.dot(
                sel, jnp.concatenate([a.astype(jnp.bfloat16) for a in around], axis=1), preferred_element_type=jnp.float32
            )
            balanced = jnp.concatenate(
                [
                    (a[HW : HW + channels] - total[:, n * samples : (n + 1) * samples] * inv).astype(jnp.bfloat16)
                    for n, a in enumerate(around)
                ],
                axis=0,
            )
            ram_sum = jnp.dot(jnp.abs(balanced), ram, preferred_element_type=jnp.float32)
            envelope = ram_sum * raminv + EPSILON
            normalized = (balanced.astype(jnp.float32) / envelope).astype(jnp.bfloat16)
            spectra = lax.dot_general(table, normalized, (((1,), (1,)), ((), ())), preferred_element_type=jnp.float32)
            re, im = spectra[:bins], spectra[bins:]
            power = re * re + im * im
            first = power.astype(jnp.bfloat16)
            second = (power - first.astype(jnp.float32)).astype(jnp.bfloat16)
            pieces = jnp.concatenate([first, second], axis=0)
            band_sum = jnp.dot(band, pieces, preferred_element_type=jnp.float32)
            for n, w in enumerate(group):
                part = slice(n * channels, (n + 1) * channels)
                scale = lax.rsqrt(jnp.maximum(band_sum[:, part] * bandinv, FLOOR))
                wide_rows[pl.ds(w, bins, stride=PITCH), :] = re[:, part] * scale
                wide_rows[pl.ds(bins * PITCH + w, bins, stride=PITCH), :] = im[:, part] * scale
        out_ref[:, :, done : done + step, :] = wide[:, :step, :].reshape(2, bins, step, channels).astype(out_ref.dtype)


def borders_kernel(early, x_ref, first_ref, rest_ref, inner_ref, sems):
    channels, windows, _ = x_ref.shape
    late = windows - early
    top = channels - HW
    outer = lax.axis_index("blk") % 2 * top
    inner = top - outer
    copies = [
        pltpu.make_async_copy(x_ref.at[pl.ds(outer, HW), pl.ds(0, early), :], first_ref, sems.at[0]),
        pltpu.make_async_copy(x_ref.at[pl.ds(inner, HW)], inner_ref, sems.at[1]),
        pltpu.make_async_copy(x_ref.at[pl.ds(outer, HW), pl.ds(early, late), :], rest_ref, sems.at[2]),
    ]
    for copy in copies:
        copy.start()
    for copy in copies:
        copy.wait()


def borders(traces, early):
    _, windows, samples = traces.shape
    shape = lambda n: jax.ShapeDtypeStruct((HW, n, samples), traces.dtype)
    return pl.pallas_call(
        functools.partial(borders_kernel, early),
        in_specs=[pl.BlockSpec(memory_space=pl.ANY)],
        out_specs=[pl.BlockSpec(memory_space=pltpu.VMEM)] * 3,
        out_shape=[shape(early), shape(windows - early), shape(windows)],
        scratch_shapes=[pltpu.SemaphoreType.DMA((3,))],
        cost_estimate=pl.CostEstimate(flops=1, bytes_accessed=1, transcendentals=0),
        name="borders",
    )(traces)


def prepare(x, halos, first, windows, consts):
    channels, _, samples = x.shape
    bins = samples // 2
    operands = [x, *[a for a, _ in halos], *consts]
    inside = pl.BlockSpec(memory_space=pltpu.VMEM)
    return pl.pallas_call(
        functools.partial(prepare_kernel, first, [start for _, start in halos]),
        in_specs=[inside] * len(operands),
        out_specs=inside,
        out_shape=jax.ShapeDtypeStruct((2, bins, windows, channels), jnp.bfloat16),
        scratch_shapes=[
            pltpu.VMEM((channels + 2 * HW, PITCH, samples), jnp.float32),
            pltpu.VMEM((2 * bins, PITCH, channels), jnp.float32),
        ],
        compiler_params=pltpu.CompilerParams(vmem_limit_bytes=VMEM),
        cost_estimate=pl.CostEstimate(flops=1, bytes_accessed=1, transcendentals=0),
        name="prepare",
    )(*operands)


def correlate_kernel(n_own, scale, *refs):
    own, partner = refs[:n_own], refs[n_own : 2 * n_own]
    out_ref, wide = refs[-2:]
    step = own[0].shape[1]
    channels = own[0].shape[3]
    multiply(own, partner, 0, 0, step, scale, wide)
    for part in range(2):
        out_ref[:, 0, part] = wide[part, :, :step, :].astype(out_ref.dtype)


def multiply(own, partner, first, partner_first, bins, scale, wide):
    channels = own[0].shape[3]
    rows = wide.reshape(2, channels * PITCH, channels)
    dims = (((0,), (0,)), ((), ()))

    def whole(group, part, k):
        pieces = [ref[part, k] for ref in group]
        return pieces[0] if len(pieces) == 1 else jnp.concatenate(pieces, axis=0)

    for k in range(bins):
        a_re, a_im = whole(own, 0, first + k), whole(own, 1, first + k)
        b = jnp.concatenate([whole(partner, 0, partner_first + k), whole(partner, 1, partner_first + k)], axis=1)
        by_re = lax.dot_general(a_re, b, dims, preferred_element_type=jnp.float32)
        by_im = lax.dot_general(a_im, b, dims, preferred_element_type=jnp.float32)
        re = by_re[:, :channels] + by_im[:, channels:]
        im = by_im[:, :channels] - by_re[:, channels:]
        rows[0, pl.ds(k, channels, stride=PITCH), :] = re * scale
        rows[1, pl.ds(k, channels, stride=PITCH), :] = im * scale


def correlate(own, partner, round_index, target):
    _, total_bins, _, channels = own[0].shape
    windows = sum(a.shape[2] for a in own)
    operands = [*own, *partner, target]
    specs = [pl.BlockSpec((2, BINS_STEP, a.shape[2], channels), lambda i: (0, i, 0, 0)) for a in operands[:-1]]
    return pl.pallas_call(
        functools.partial(correlate_kernel, len(own), 1.0 / math.sqrt(windows)),
        grid=(total_bins // BINS_STEP,),
        in_specs=specs + [pl.BlockSpec(memory_space=pl.ANY)],
        out_specs=pl.BlockSpec((channels, 1, 2, BINS_STEP, channels), lambda i: (0, round_index, 0, i, 0)),
        out_shape=jax.ShapeDtypeStruct(target.shape, target.dtype),
        scratch_shapes=[pltpu.VMEM((2, channels, PITCH, channels), jnp.float32)],
        input_output_aliases={len(operands) - 1: 0},
        compiler_params=pltpu.CompilerParams(vmem_limit_bytes=VMEM),
        cost_estimate=pl.CostEstimate(flops=1, bytes_accessed=1, transcendentals=0),
        name="correlate",
    )(*operands)


def correlate_chunk_kernel(n_own, scale, first_bin, round_index, *refs):
    own, partner, far = refs[:n_own], refs[n_own : 2 * n_own], refs[2 * n_own]
    out_ref, wide, done, sems = refs[-4:]
    bins = far.shape[1]
    odd = lax.axis_index("blk") % 2 != 0
    pl.when(jnp.logical_not(odd))(lambda: multiply(own, partner, first_bin, first_bin, bins, scale, wide))
    pl.when(odd)(lambda: multiply(own, [far], first_bin, 0, bins, scale, wide))
    copies = []
    for part in range(2):
        done[part] = wide[part, :, :bins, :].astype(done.dtype)
        copies.append(
            pltpu.make_async_copy(
                done.at[part], out_ref.at[:, round_index, part, pl.ds(first_bin, bins), :], sems.at[part]
            )
        )
        copies[-1].start()
    for copy in copies:
        copy.wait()


def correlate_chunk(own, partner, round_index, first_bin, far, target, after):
    _, bins, windows, channels = far.shape
    total_bins = own[0].shape[1]
    operands = [*own, *partner, far]
    specs = [pl.BlockSpec(memory_space=pltpu.VMEM)] * len(operands)
    aliases = {}
    if target is not None:
        aliases = {len(operands): 0}
        operands.append(target)
        specs.append(pl.BlockSpec(memory_space=pl.ANY))
    operands.append(after)
    specs.append(pl.BlockSpec(memory_space=pl.ANY))
    return pl.pallas_call(
        functools.partial(
            correlate_chunk_kernel, len(own), 1.0 / math.sqrt(windows), first_bin, round_index
        ),
        in_specs=specs,
        out_specs=pl.BlockSpec(memory_space=pl.ANY),
        out_shape=jax.ShapeDtypeStruct((channels, ROUNDS, 2, total_bins, channels), jnp.bfloat16),
        scratch_shapes=[
            pltpu.VMEM((2, channels, PITCH, channels), jnp.float32),
            pltpu.VMEM((2, channels, bins, channels), jnp.bfloat16),
            pltpu.SemaphoreType.DMA((2,)),
        ],
        input_output_aliases=aliases,
        compiler_params=pltpu.CompilerParams(vmem_limit_bytes=VMEM),
        cost_estimate=pl.CostEstimate(flops=1, bytes_accessed=1, transcendentals=0),
        name="correlate_chunk",
    )(*operands)


def edges(block, total_channels, channels, samples):
    inner, outer = np.arange(channels), np.arange(channels + 2 * HW)
    offset = outer[None, :] - inner[:, None]
    near = jnp.asarray((offset >= 0) & (offset <= 2 * HW))
    at = block * channels - HW + jnp.asarray(outer, jnp.int32)
    sel = (near & (at >= 0)[None, :] & (at < total_channels)[None, :]).astype(jnp.bfloat16)
    own = block * channels + jnp.asarray(inner, jnp.int32)
    count = jnp.minimum(own, HW) + jnp.minimum(total_channels - 1 - own, HW) + 1
    inv = jnp.broadcast_to((1.0 / count.astype(jnp.float32))[:, None], (channels, samples))
    return [sel, inv]


def tables(channels, samples, bands):
    bins = samples // 2
    sample = np.arange(samples)
    near = np.abs(sample[:, None] - sample[None, :]) <= RAM_HALF
    ram = near.astype(ml_dtypes.bfloat16)
    raminv = (1.0 / near.sum(axis=0, dtype=np.float32)).astype(np.float32)[None, :]
    phase = 2.0 * math.pi / samples * (np.arange(1, bins + 1)[:, None] * sample[None, :] % samples)
    table = (np.concatenate([np.cos(phase), -np.sin(phase)], axis=0) / math.sqrt(samples)).astype(ml_dtypes.bfloat16)
    same = bands[:, None] == bands[None, :]
    size = jnp.sum(same.astype(jnp.float32), axis=1, keepdims=True)
    band = jnp.tile(same.astype(jnp.bfloat16), (1, 2))
    bandinv = jnp.broadcast_to(1.0 / size, (bins, channels))
    return [jnp.asarray(ram), jnp.asarray(raminv), jnp.asarray(table), band, bandinv]


def per_device(traces, bands):
    channels, windows, samples = traces.shape
    bins = samples // 2
    count = lax.axis_size("blk")
    block = lax.axis_index("blk")
    swap = [(i, i ^ 1) for i in range(count)]
    cross = [(i, i + 1 if i % 2 else i - 1) for i in range(1, count - 1)]
    first_pairs = [((i + 2) % count, i) if i % 2 == 0 else (i, i) for i in range(count)]
    second_pairs = [((i + 2) % count, i) for i in range(1, count, 2)]
    early = HALO_STEPS * STEP

    outer_first, outer_rest, inner = borders(traces, early)
    above_first = lax.ppermute(outer_first, "blk", [(i + 1, i) for i in range(1, count - 1, 2)])
    below_first = lax.ppermute(outer_first, "blk", [(i, i + 1) for i in range(1, count - 1, 2)])
    beside = lax.ppermute(inner, "blk", swap)
    across_rest = lax.ppermute(outer_rest, "blk", cross)
    consts = edges(block, channels * count, channels, samples) + tables(channels, samples, bands)

    own, held = [], []
    at = 0
    for n, size in enumerate(CHUNKS):
        if n == 1:
            below_first, across_rest, own[0] = lax.optimization_barrier((below_first, across_rest, own[0]))
        elif n > 1:
            across_rest, own[-1], held[n - 2] = lax.optimization_barrier((across_rest, own[-1], held[n - 2]))
        if at < early:
            halos = [(below_first, at), (beside, at), (beside, at), (above_first, at)]
        else:
            halos = [(across_rest, at - early), (beside, at), (beside, at), (across_rest, at - early)]
        x, first = (traces[:, : size * STEP], 0) if n == 0 else (traces, at)
        own.append(prepare(x, halos, first, size * STEP, consts))
        held.append(lax.ppermute(own[-1], "blk", first_pairs))
        at += size * STEP
    token = lax.ppermute(held[TOKEN][0, 0, :STEP], "blk", swap)
    far = []
    for first in range(0, bins, BINS_STEP):
        mine = jnp.concatenate([c[:, first : first + BINS_STEP] for c in own], axis=2)
        mine, token = lax.optimization_barrier((mine, token))
        far.append(lax.ppermute(mine, "blk", second_pairs))
    other = []
    for n in range(len(held)):
        if n in AFTER:
            held[n], other[AFTER[n]] = lax.optimization_barrier((held[n], other[AFTER[n]]))
        other.append(lax.ppermute(held[n], "blk", swap))
    out = None
    for n, first in enumerate(range(0, bins, BINS_STEP)):
        if n == FIRST_ROUND_AFTER:
            out = correlate(own, other, 0, out)
        out = correlate_chunk(own, held, 1, first, far[n], out, token)
    return out


def solution(mesh):
    placed = (P("blk", None, None), P())
    return jax.shard_map(
        per_device,
        mesh=mesh,
        in_specs=placed,
        out_specs=P("blk", None, None, None, None),
        check_vma=False,
    )
```
